32 devices in a mesh: groups: 2 (over x), pairs: 16 (over z, y, core).
Axes of the slice: x: 2, y: 2, z: 4, core: 2. Of those that a mesh axis runs over, the one named last changes fastest.
Arguments:
- traces: bfloat16 [128, 3, 4096], P(('groups', 'pairs')), parts along dimension 0, may hold values from -6 to 6
- gaps: int32 [128, 2], P(('groups', 'pairs')), parts along dimension 0, may hold values 0 or 1
- assign: int32 [128], P('groups'), parts along dimension 0, may hold values from 0 to 3, as said below
- target: int32 [32], P('groups'), parts along dimension 0, may hold values from 0 to 3, as said below
Outputs:
- correlations: bfloat16 [128, 16, 2, 9, 256], P(('groups', 'pairs')), parts along dimension 0
- energy: float32 [128, 9], P(('groups', 'pairs')), parts along dimension 0
The draws below stay inside these ranges and needn't reach their ends.
There are 2 independent parts, one for each index of `groups`. The reference program is written for one: setup_inputs(seed, part) draws one part's arguments, and reference() takes and returns one part's arrays. A program takes and returns all parts, laid end to end along the dimension named above; each array names one. Nothing has to cross between parts.
Inputs may be any that keep to these rules, and one draw needn't show every extreme that they name: `assign`: the 4 stations of one owner name at most 2 stations of any block; in every draw one block takes exactly 2 stations of every owner. `target`: in every draw some owner names the block that takes 2 stations of every owner.
All inputs are finite; a program needn't handle non-finite values. No bound on the sum of `gaps` on one device may be relied on, other than what follows from the above.
Results may differ from the reference program's by a relative error of at most 0.0075.
Values may be sent and summed in bfloat16 or wider, within the bound.
A program may use at most 128 MiB of HBM per device.

```python
import math
import jax
import jax.numpy as jnp
from jax import lax

STA_DEV = 4
WINDOWS = 2
SEG = 2048
FREQ = 512
FLO = 64
LAGS = 256
HALF = 21
CAP = 2
BLOCKS = 4
OWNERS = 16
STATIONS = 64
N_PAIRS = 16


def block_plan(key):
    base = jax.random.fold_in(key, 4242)
    hot_key, owner_key, target_key, holder_key = jax.random.split(base, 4)
    hottest = jax.random.randint(hot_key, (), 0, BLOCKS)
    others = jnp.arange(BLOCKS - 1, dtype=jnp.int32)
    others = jnp.where(others >= hottest, others + 1, others)
    pool = jnp.repeat(others, CAP)

    def one_owner(owner_seed):
        first_seed, second_seed = jax.random.split(owner_seed)
        chosen = jax.random.permutation(first_seed, pool)[:STA_DEV - CAP]
        filled = jnp.concatenate([jnp.full((CAP,), hottest, jnp.int32), chosen.astype(jnp.int32)])
        return jax.random.permutation(second_seed, filled)
    assigned = jax.vmap(one_owner)(jax.random.split(owner_key, OWNERS)).reshape(-1)
    targets = jax.random.randint(target_key, (OWNERS,), 0, BLOCKS)
    holder = jax.random.randint(holder_key, (), 0, OWNERS)
    targets = jnp.where(jnp.arange(OWNERS) == holder, hottest, targets)
    return (assigned.astype(jnp.int32), targets.astype(jnp.int32))


def draw_assign(key, part):
    return block_plan(key)[0]


def draw_target(key, part):
    return block_plan(key)[1]


def with_ends(values, rng, least, largest):
    index_at = [jax.random.randint(jax.random.fold_in(rng, axis), (), 0, length) for axis, length in enumerate(values.shape)]
    main_axis = values.shape.index(max(values.shape))
    beside = index_at[:main_axis] + [(index_at[main_axis] + 1) % values.shape[main_axis]] + index_at[main_axis + 1:]
    return values.at[tuple(index_at)].set(least).at[tuple(beside)].set(largest)


def shard_levels(key, shape, shards, low, top_value):
    def one(axis_at, parts):
        draws = jax.random.uniform(jax.random.fold_in(jax.random.fold_in(key, 6), axis_at), (parts,), jnp.float32, low / len(shards), top_value / len(shards))
        return jnp.repeat(jnp.exp(draws), shape[axis_at] // parts).reshape((-1,) + (1,) * (len(shape) - axis_at - 1))

    level = one(*shards[0])
    for cut in shards[1:]:
        level = level * one(*cut)
    return level


def normal_values(key, shape, width, bound, pieces=(), kind=jnp.bfloat16):
    array = width * jax.random.normal(key, shape, jnp.float32)
    if pieces:
        array = array * shard_levels(key, shape, pieces, -0.22, 0.18)
    return jnp.clip(array, -bound, bound).astype(kind)


def setup_inputs(seed: int = 0, part: int = 0) -> dict:
    arg_keys = jax.random.split(jax.random.key(seed), 5)
    part_keys = jax.random.split(jax.random.fold_in(arg_keys[4], part), 5)
    return {
        "traces": normal_values(part_keys[0], (STATIONS, 3, WINDOWS * SEG), 1.0, 6.0, ((0, 16),)),
        "gaps": with_ends((jax.random.randint(part_keys[1], (STATIONS, WINDOWS), 0, 4) < 3).astype(jnp.int32), jax.random.fold_in(part_keys[1], 1), 0, 1),
        "assign": draw_assign(jax.random.fold_in(jax.random.fold_in(arg_keys[4], part), 71), part),
        "target": draw_target(jax.random.fold_in(jax.random.fold_in(arg_keys[4], part), 71), part),
    }


def dft_table():
    samples = jnp.arange(SEG, dtype=jnp.int32)[:, None]
    bins = FLO + jnp.arange(FREQ, dtype=jnp.int32)[None, :]
    phase = jnp.mod(samples * bins, SEG).astype(jnp.float32) * (2.0 * math.pi / SEG)
    return jnp.concatenate([jnp.cos(phase), -jnp.sin(phase)], axis=1).astype(jnp.bfloat16)

def lag_table():
    bins = FLO + jnp.arange(FREQ, dtype=jnp.int32)[:, None]
    shifts = jnp.arange(LAGS, dtype=jnp.int32)[None, :] - LAGS // 2
    phase = jnp.mod(bins * shifts, SEG).astype(jnp.float32) * (2.0 * math.pi / SEG)
    return jnp.concatenate([jnp.cos(phase), -jnp.sin(phase)], axis=0).astype(jnp.bfloat16)

def smooth_band():
    column = jnp.arange(FREQ, dtype=jnp.int32)
    band = (jnp.abs(column[:, None] - column[None, :]) <= HALF).astype(jnp.float32)
    return (band, lax.optimization_barrier(jnp.sum(band, axis=0)))

def whiten_all(traces, gaps):
    stations = traces.shape[0]
    windows = gaps.shape[1]
    segments = traces.reshape(stations * 3 * windows, SEG)
    spectra = jnp.dot(segments, dft_table(), preferred_element_type=jnp.float32)
    spectra = spectra.reshape(stations, 3, windows, 2, FREQ)
    power = lax.optimization_barrier(jnp.sum(spectra * spectra, axis=(1, 3))) / 3.0
    band, bin_count = smooth_band()
    smooth = jnp.dot(power.reshape(-1, FREQ), band, precision=lax.Precision.HIGHEST)
    smooth = smooth.reshape(stations, windows, FREQ) / bin_count
    factor = gaps.astype(jnp.float32)[:, :, None] / jnp.sqrt(smooth + 1e-06)
    return (spectra * factor[:, None, :, None, :]).astype(jnp.bfloat16)

def station_ranks(owner_assign):
    own_count = owner_assign.shape[1]
    same = owner_assign[:, :, None] == owner_assign[:, None, :]
    order = jnp.arange(own_count, dtype=jnp.int32)
    before = order[:, None] < order[None, :]
    return lax.optimization_barrier(jnp.sum((same & before[None, :, :]).astype(jnp.int32), axis=1))

def correlate_block(whitened, own_mask, partner, partner_mask):
    own_count = whitened.shape[0]
    slot_count = partner.shape[0]
    real_part = partner[:, :, :, 0]
    imag_part = partner[:, :, :, 1]
    quad = jnp.stack([jnp.stack([real_part, imag_part], 3), jnp.stack([-imag_part, real_part], 3)], 4)
    cross = jnp.einsum('icwrf,jdwrof->ijcdof', whitened.astype(jnp.float32), quad.astype(jnp.float32))
    cross = cross.astype(jnp.bfloat16)
    lagged = jnp.dot(cross.reshape(-1, 2 * FREQ), lag_table(), preferred_element_type=jnp.float32)
    lagged = lagged.reshape(own_count, slot_count, 9, LAGS)
    counts = jnp.dot(own_mask, partner_mask.T, precision=lax.Precision.HIGHEST)
    scale = 1.0 / (jnp.maximum(counts, 1.0) * math.sqrt(FREQ))
    return (lagged * scale[:, :, None, None]).astype(jnp.bfloat16)

def reference(traces, gaps, assign, target):
    owners = N_PAIRS
    own_count = STA_DEV
    windows = gaps.shape[1]
    whitened = whiten_all(traces, gaps).reshape(owners, own_count, 3, windows, 2, FREQ)
    masks = gaps.astype(jnp.float32).reshape(owners, own_count, windows)
    owner_assign = assign.reshape(owners, own_count)
    ranks = station_ranks(owner_assign)
    flat_rows = whitened.reshape(owners, own_count, -1).astype(jnp.float32)
    slot_ids = jnp.arange(CAP, dtype=jnp.int32)

    def per_owner(inputs):
        own_white, own_mask, wanted = inputs
        selection = ((owner_assign == wanted)[:, None, :] & (ranks[:, None, :] == slot_ids[None, :, None])).astype(jnp.float32)
        partner = jnp.einsum('ecs,esr->ecr', selection, flat_rows).astype(jnp.bfloat16)
        partner_mask = jnp.einsum('ecs,esw->ecw', selection, masks)
        block = correlate_block(own_white, own_mask, partner.reshape(owners * CAP, 3, windows, 2, FREQ), partner_mask.reshape(owners * CAP, windows))
        slot_energy = lax.optimization_barrier(jnp.sum(jnp.square(block.astype(jnp.float32)), axis=(0, 3))).reshape(owners, CAP, 9)
        share = jnp.einsum('ecs,ecq->esq', selection, slot_energy, precision=lax.Precision.HIGHEST)
        return (block.reshape(own_count, owners, CAP, 9, LAGS), share)
    blocks, shares = lax.map(per_owner, (whitened, masks, target))
    energy = lax.optimization_barrier(jnp.sum(shares, axis=0)).reshape(owners * own_count, 9) / float(owners * LAGS)
    return (blocks.reshape(owners * own_count, owners, CAP, 9, LAGS), energy)
```

```python
import functools
import math

import jax
import jax.numpy as jnp
import numpy as np
from jax import lax
from jax.experimental import pallas as pl
from jax.experimental.pallas import tpu as pltpu
from jax.sharding import PartitionSpec as P

SEG = 2048
FREQ = 512
FLO = 64
LAGS = 256
HALF = 21
CAP = 2
LANE = 128
PLANE = 4


def tables():
    step = np.float32(2.0 * math.pi / SEG)
    bins = FLO + np.arange(FREQ)
    phase = ((np.arange(SEG)[:, None] * bins[None, :]) % SEG).astype(np.float32) * step
    dft = np.concatenate([np.cos(phase), -np.sin(phase)], axis=1)
    shifts = np.arange(LAGS) - LAGS // 2
    phase = ((bins[:, None] * shifts[None, :]) % SEG).astype(np.float32) * step
    lag = np.concatenate([np.cos(phase), -np.sin(phase)], axis=0)
    return jnp.asarray(dft, jnp.bfloat16), jnp.asarray(lag, jnp.bfloat16)


def pick(assign_ref, target_ref, owner, wanted, own):
    block = target_ref[wanted]
    seen = jnp.int32(0)
    slots = [jnp.int32(-1)] * CAP
    for s in range(own):
        hit = (assign_ref[owner * own + s] == block).astype(jnp.int32)
        for c in range(CAP):
            slots[c] = jnp.where(hit * (seen == c).astype(jnp.int32) == 1, s, slots[c])
        seen = seen + hit
    return slots


def kernel(
    owners, own, wins, traces_ref, gaps_ref, assign_ref, target_ref, dft_ref, lag_ref,
    corr_ref, energy_ref,
    gath, ownx, part, cross, lagged, esend, erecv,
    zs, zr, ys, yr, cs, cr, es, er,
):
    me = lax.axis_index("pairs")
    planes = owners // PLANE
    z = me // PLANE
    core = me % 2
    peer = me + 1 - 2 * core
    yy = (me // 2) % 2
    across = me + 2 - 4 * yy
    f32, bf16 = jnp.float32, jnp.bfloat16
    rows = 2 * 3 * wins * own
    grp = own * CAP
    prow = 2 * 3 * wins * grp
    chunks = FREQ // LANE
    tail = chunks * rows

    barrier = pltpu.get_barrier_semaphore()

    def greet(k, carry):
        pl.semaphore_signal(barrier, inc=1, device_id={"pairs": (me + k) % owners},
                            device_id_type=pl.DeviceIdType.MESH)
        return carry

    lax.fori_loop(1, owners, greet, 0)

    pieces = []
    for a in range(3):
        seg = traces_ref[a].astype(f32)
        pieces += [seg[:, w * SEG:(w + 1) * SEG] for w in range(wins)]
    x = jnp.concatenate(pieces, axis=0).astype(bf16)
    spec = jnp.dot(x, dft_ref[...], preferred_element_type=f32)
    sq = spec * spec
    sq = sq[:, :FREQ] + sq[:, FREQ:]
    wi = wins * own
    power = (sq[:wi] + sq[wi:2 * wi] + sq[2 * wi:]) / 3.0
    wide = FREQ + LANE
    padded = jnp.concatenate([power, jnp.zeros((wi, LANE), f32)], axis=1)
    need, width, done, total, cur = 2 * HALF + 1, 1, 0, None, padded
    while width <= need:
        if need & width:
            term = cur if done == 0 else pltpu.roll(cur, done, 1)
            total = term if total is None else total + term
            done += width
        width *= 2
        if width <= need:
            cur = cur + pltpu.roll(cur, width // 2, 1)
    total = pltpu.roll(total, wide - HALF, 1)[:, :FREQ]
    col = lax.broadcasted_iota(jnp.int32, (wi, FREQ), 1)
    members = jnp.minimum(col + HALF, FREQ - 1) - jnp.maximum(col - HALF, 0) + 1
    smooth = total / members.astype(f32)
    row = lax.broadcasted_iota(jnp.int32, (wi, LANE), 0)
    flags = jnp.zeros((wi, LANE), f32)
    for w in range(wins):
        for i in range(own):
            flags = jnp.where(row == w * own + i, gaps_ref[w, i].astype(f32), flags)
    factor = jnp.concatenate([flags] * chunks, axis=1) / jnp.sqrt(smooth + 1e-6)
    white = jnp.concatenate(
        [spec[a * wi:(a + 1) * wi, p * FREQ:(p + 1) * FREQ] * factor for p in range(2) for a in range(3)], axis=0
    ).astype(bf16)
    for j in range(chunks):
        gath[me, j * rows:(j + 1) * rows] = white[:, j * LANE:(j + 1) * LANE]
    gath[me, tail:] = jnp.concatenate([flags, jnp.zeros((16 - wi, LANE), f32)], axis=0).astype(bf16)

    pl.semaphore_wait(barrier, owners - 1)

    def send(block, to, s_sem, r_sem):
        return pltpu.make_async_remote_copy(
            src_ref=gath.at[block], dst_ref=gath.at[block], send_sem=s_sem, recv_sem=r_sem,
            device_id={"pairs": to}, device_id_type=pl.DeviceIdType.MESH)

    def along(block, k):
        return send(block, (me + k * PLANE) % owners, zs.at[k], zr.at[k])

    def over(block, k):
        return send(block, across, ys.at[k], yr.at[k])

    def beside(block, k, half):
        return send(block, peer, cs.at[k, half], cr.at[k, half])

    def column(k):
        return (me - k * PLANE + owners) % owners

    def moved(block):
        return block + 2 - 4 * yy

    def turned(block):
        return block + 1 - 2 * core

    def send_own(k, carry):
        along(me, k).start()
        return carry

    lax.fori_loop(1, planes, send_own, 0)
    over(me, 0).start()
    beside(me, 0, 0).start()

    r_iota = lax.broadcasted_iota(jnp.int32, (prow, rows), 0)
    c_iota = lax.broadcasted_iota(jnp.int32, (prow, rows), 1)
    double = ((r_iota // grp == c_iota // own) & ((r_iota % grp) // CAP == c_iota % own))
    ownx[...] = jnp.dot(double.astype(f32).astype(bf16), white, preferred_element_type=f32)

    gr = lax.broadcasted_iota(jnp.int32, (grp, 16), 0)
    gc = lax.broadcasted_iota(jnp.int32, (grp, 16), 1)
    own_flags = jnp.zeros((grp, 16), f32)
    for w in range(wins):
        for i in range(own):
            own_flags = jnp.where((gr // CAP == i) & (gc // own == w), gaps_ref[w, i].astype(f32), own_flags)

    lane = lax.broadcasted_iota(jnp.int32, (grp, LANE), 1)

    def correlate(k):
        zg = (z - k + planes) % planes
        first = zg * PLANE
        base_r = lax.broadcasted_iota(jnp.int32, (prow, PLANE * rows), 0)
        base_c = lax.broadcasted_iota(jnp.int32, (prow, PLANE * rows), 1)
        odd = base_r % CAP == 1
        select, scales = [], []
        for j in range(PLANE):
            slots = pick(assign_ref, target_ref, first + j, me, own)
            station = jnp.where(odd, slots[1], slots[0])
            hit = (base_c // own == j * (rows // own) + base_r // grp) & (base_c % own == station)
            select.append(hit.astype(f32))
            station = jnp.where(gr % CAP == 1, slots[1], slots[0])
            weight = jnp.where(gc % own == station, own_flags, 0.0).astype(bf16)
            count = jnp.dot(weight, gath[first + j, tail:], preferred_element_type=f32)
            scales.append(1.0 / (jnp.maximum(count, 1.0) * math.sqrt(FREQ)))
        select = jnp.concatenate(select, axis=0).astype(bf16)
        data = jnp.concatenate(
            [
                jnp.concatenate([gath[first + j, n * rows:(n + 1) * rows] for n in range(chunks)], axis=1)
                for j in range(PLANE)
            ],
            axis=0,
        )
        part[...] = jnp.dot(select, data, preferred_element_type=f32)
        half = 3 * wins * grp
        for pair in range(PLANE // 2):
            for n in range(chunks):
                cols = slice(n * LANE, (n + 1) * LANE)
                for b in range(3):
                    for a in range(3):
                        res, ims = [], []
                        for par in range(2):
                            off = (pair * 2 + par) * prow
                            re = im = None
                            for w in range(wins):
                                oa = (a * wins + w) * grp
                                ob = off + (b * wins + w) * grp
                                wr, wm = ownx[oa:oa + grp, cols], ownx[half + oa:half + oa + grp, cols]
                                pr, pm = part[ob:ob + grp, cols], part[half + ob:half + ob + grp, cols]
                                r1, i1 = wr * pr + wm * pm, wm * pr - wr * pm
                                re, im = (r1, i1) if re is None else (re + r1, im + i1)
                            res.append(re)
                            ims.append(im)
                        at = (pair * 9 + 3 * a + b) * 2 * grp
                        cross[at:at + 2 * grp, cols] = jnp.concatenate(res, axis=0).astype(bf16)
                        cross[at:at + 2 * grp, FREQ + n * LANE:FREQ + (n + 1) * LANE] = (
                            jnp.concatenate(ims, axis=0).astype(bf16))
        lagged[...] = jnp.dot(cross[...], lag_ref[...], preferred_element_type=f32)
        for j in range(PLANE):
            e = first + j
            scale = jnp.concatenate([scales[j]] * (LAGS // LANE), axis=1)
            energies = jnp.zeros((grp, LANE), f32)
            for q in range(9):
                at = (((j // 2) * 9 + q) * 2 + j % 2) * grp
                value = (lagged[at:at + grp] * scale).astype(bf16)
                for i in range(own):
                    corr_ref[i, e, q] = value[CAP * i:CAP * (i + 1)]
                wide_value = value.astype(f32)
                energy = jnp.sum(wide_value * wide_value, axis=1, keepdims=True)
                energies = jnp.where(lane == q, energy, energies)
            esend[e] = energies

            @pl.when(e != me)
            def _():
                energy_copy(e, me).start()

            @pl.when(e == me)
            def _():
                erecv[me] = energies

    def energy_copy(to, source):
        return pltpu.make_async_remote_copy(
            src_ref=esend.at[to], dst_ref=erecv.at[source], send_sem=es.at[to], recv_sem=er.at[source],
            device_id={"pairs": to}, device_id_type=pl.DeviceIdType.MESH)

    def finish(k):
        block = column(k)
        over(moved(block), k).wait_recv()
        beside(moved(block), k, 1).start()
        beside(turned(block), k, 0).wait_recv()
        beside(turned(moved(block)), k, 1).wait_recv()
        correlate(k)

    finish(0)

    def forward(k, carry):
        block = column(k)
        along(block, k).wait_recv()
        over(block, k).start()
        beside(block, k, 0).start()
        return carry

    lax.fori_loop(1, planes, forward, 0)

    def rest(k, carry):
        finish(k)
        return carry

    lax.fori_loop(1, planes, rest, 0)

    cell = lax.broadcasted_iota(jnp.int32, (8, owners * grp), 1)
    chosen = jnp.full((8, owners * grp), -1, jnp.int32)

    def choose(p, chosen):
        slots = pick(assign_ref, target_ref, me, p, own)
        return jnp.where(cell // grp == p, jnp.where(cell % CAP == 1, slots[1], slots[0]), chosen)

    chosen = lax.fori_loop(0, owners, choose, chosen)
    pick_out = (chosen == lax.broadcasted_iota(jnp.int32, (8, owners * grp), 0)).astype(f32)

    def collect(k, carry):
        energy_copy(me, (me + k) % owners).wait_recv()
        return carry

    lax.fori_loop(1, owners, collect, 0)
    result = jnp.dot(pick_out, erecv[...].reshape(owners * grp, LANE),
                     precision=lax.Precision.HIGHEST, preferred_element_type=f32)
    energy_ref[...] = result[:own, :9] / float(owners * LAGS)

    def drain(k, carry):
        along(me, k).wait_send()
        return carry

    lax.fori_loop(1, planes, drain, 0)

    def drain_near(k, carry):
        over(me, k).wait_send()
        beside(me, k, 0).wait_send()
        beside(me, k, 1).wait_send()
        return carry

    lax.fori_loop(0, planes, drain_near, 0)

    def drain_energy(k, carry):
        energy_copy((me + k) % owners, me).wait_send()
        return carry

    lax.fori_loop(1, owners, drain_energy, 0)


def solution(mesh):
    owners = mesh.shape["pairs"]

    def on_device(traces, gaps, assign, target):
        own, wins = gaps.shape
        planes = owners // PLANE
        rows = 2 * 3 * wins * own
        grp = own * CAP
        dft, lag = tables()
        vmem = pl.BlockSpec(memory_space=pltpu.VMEM)
        smem = pl.BlockSpec(memory_space=pltpu.SMEM)
        dma = pltpu.SemaphoreType.DMA
        corr, energy = pl.pallas_call(
            functools.partial(kernel, owners, own, wins),
            out_shape=(
                jax.ShapeDtypeStruct((own, owners, 9, CAP, LAGS), jnp.bfloat16),
                jax.ShapeDtypeStruct((own, 9), jnp.float32),
            ),
            in_specs=[vmem, smem, smem, smem, vmem, vmem],
            out_specs=(vmem, vmem),
            scratch_shapes=[
                pltpu.VMEM((owners, (FREQ // LANE) * rows + 16, LANE), jnp.bfloat16),
                pltpu.VMEM((rows * CAP, FREQ), jnp.float32),
                pltpu.VMEM((PLANE * rows * CAP, FREQ), jnp.float32),
                pltpu.VMEM((PLANE * 9 * grp, 2 * FREQ), jnp.bfloat16),
                pltpu.VMEM((PLANE * 9 * grp, LAGS), jnp.float32),
                pltpu.VMEM((owners, grp, LANE), jnp.float32),
                pltpu.VMEM((owners, grp, LANE), jnp.float32),
                dma((planes,)), dma((planes,)), dma((planes,)), dma((planes,)),
                dma((planes, 2)), dma((planes, 2)), dma((owners,)), dma((owners,)),
            ],
            compiler_params=pltpu.CompilerParams(
                collective_id=0, has_side_effects=True, vmem_limit_bytes=48 * 1024 * 1024),
        )(traces.transpose(1, 0, 2), gaps.T, assign, target, dft, lag)
        return corr.transpose(0, 1, 3, 2, 4), energy

    in_specs = (
        P(("groups", "pairs"), None, None),
        P(("groups", "pairs"), None),
        P("groups"),
        P("groups"),
    )
    out_specs = (P(("groups", "pairs"), None, None, None, None), P(("groups", "pairs"), None))
    return jax.shard_map(
        on_device, mesh=mesh, in_specs=in_specs, out_specs=out_specs, check_vma=False
    )
```
